512 devices in a mesh: row: 32 (over z, core), col: 16 (over x, y).
Axes of the slice: x: 4, y: 4, z: 16, core: 2. Of those that a mesh axis runs over, the one named last changes fastest.
Arguments:
- tensor: float32 [16, 8192, 4096], P(None, 'row', 'col'), may hold values from -270 to 270
- factor_b: float32 [64, 4096], P(None, 'col'), may hold values from -6 to 6
- factor_c: float32 [16, 64], replicated, may hold values from -6 to 6
Outputs:
- result_a: float32 [64, 8192], P(None, 'row')
- result_b: float32 [64, 4096], P(None, 'col')
- column_scales: float32 [2, 64], replicated
The draws below stay inside these ranges and needn't reach their ends.
All inputs are finite; a program needn't handle non-finite values.
Results may differ from the reference program's by a relative error of at most 0.0003.
Values sent between devices are 32-bit elements; how exact they have to be, the bound alone decides.
A program may use at most 64 MiB of HBM per device.

```python
import math
import jax
import jax.numpy as jnp
from jax import lax

K = 16
R = 64
SWEEPS = 3
NI = 8192
NJ = 4096


def draw_tensor(key, part):
    key = jax.random.fold_in(key, 1)
    key_row, key_col, key_noise = jax.random.split(key, 3)
    row_pos = jnp.arange(NI, dtype=jnp.float32) / NI
    col_pos = jnp.arange(NJ, dtype=jnp.float32) / NJ
    row_scale = (1.0 + 2.0 * row_pos) * jnp.exp(jax.random.uniform(key_row, (NI,), jnp.float32, 0.0, math.log(10.0)))
    col_scale = (1.0 + 2.0 * col_pos) * jnp.exp(jax.random.uniform(key_col, (NJ,), jnp.float32, 0.0, math.log(10.0)))
    noise = jnp.clip(jax.random.normal(key_noise, (K, NI, NJ), jnp.float32), -6.0, 6.0)
    return (0.05 * noise * row_scale[None, :, None] * col_scale[None, None, :]).astype(jnp.float32)


def shard_levels(own_key, shape, shards, smallest, high):
    factor_of, own = 1.0, jax.random.fold_in(own_key, 6)
    for position, blocks in shards:
        heights = jnp.exp(jax.random.uniform(jax.random.fold_in(own, position), (blocks,), jnp.float32, smallest / len(shards), high / len(shards)))
        factor_of = factor_of * jnp.repeat(heights, shape[position] // blocks).reshape([-1 if axis == position else 1 for axis in range(len(shape))])
    return factor_of


def normal_values(key, extent, width, limit, cuts=(), kind=jnp.bfloat16):
    gain = shard_levels(key, extent, cuts, -0.22, 0.18) if cuts else 1.0
    drawn = jax.random.normal(key, extent, jnp.float32) * width * gain
    return jnp.minimum(jnp.maximum(drawn, -limit), limit).astype(kind)


def setup_inputs(seed: int = 0) -> dict:
    keys = jax.random.split(jax.random.key(seed), 4)
    return {
        "tensor": draw_tensor(jax.random.fold_in(keys[3], 71), 0),
        "factor_b": normal_values(keys[1], (R, NJ), 1.0, 6.0, ((1, 16),), jnp.float32),
        "factor_c": normal_values(keys[2], (K, R), 1.0, 6.0, (), jnp.float32),
    }


epsilon = 1e-06

def gram_of(factor):
    return jnp.dot(factor.astype(jnp.float32), factor.T.astype(jnp.float32), precision=lax.Precision.HIGHEST, preferred_element_type=jnp.float32)

def update(mttkrp, system, count):
    lower = jnp.linalg.cholesky(system)
    solved = jax.scipy.linalg.cho_solve((lower, True), mttkrp)
    scales = jnp.sqrt(lax.optimization_barrier(jnp.sum(solved * solved, axis=1)) / count + epsilon)
    return (solved / scales[:, None], scales)

def reference(tensor, factor_b, factor_c):
    highest = lax.Precision.HIGHEST
    identity = jnp.eye(R, dtype=jnp.float32)
    gram_c = jnp.dot(factor_c.T.astype(jnp.float32), factor_c.astype(jnp.float32), precision=highest, preferred_element_type=jnp.float32)
    current_b = factor_b
    gram_b = gram_of(current_b)
    current_a = jnp.zeros((R, NI), jnp.float32)
    scales_a = jnp.zeros((R,), jnp.float32)
    scales_b = jnp.zeros((R,), jnp.float32)
    for sweep in range(SWEEPS):
        inner = jnp.einsum('kij,rj->kir', tensor, current_b, precision=highest)
        mttkrp_a = jnp.einsum('kir,kr->ri', inner, factor_c, precision=highest)
        current_a, scales_a = update(mttkrp_a, gram_c * gram_b + NJ * identity, NI)
        gram_a = gram_of(current_a)
        outer = jnp.einsum('ri,kij->krj', current_a, tensor, precision=highest)
        mttkrp_b = jnp.einsum('krj,kr->rj', outer, factor_c, precision=highest)
        current_b, scales_b = update(mttkrp_b, gram_c * gram_a + NI * identity, NJ)
        gram_b = gram_of(current_b)
    return (current_a, current_b, jnp.stack([scales_a, scales_b]))
```

```python
import jax
import jax.numpy as jnp
from jax import lax
from jax.experimental import pallas as pl
from jax.experimental.pallas import tpu as pltpu
from jax.sharding import PartitionSpec as P

SWEEPS = 3
EPSILON = 1e-06
MESH = pl.DeviceIdType.MESH
HIGHEST = lax.Precision.HIGHEST
F32 = jnp.float32
BF16 = jnp.bfloat16

CHIPS = 16
COLS = 16
SIDE = 4

SERVED = ((0, 0), (1, 0), (3, 0), (0, 1), (0, 3), (2, 0), (1, 1), (1, 3))
WINDOW = (-4, -3, 3, -2, 2, -1, 1, 0)


def ring(offset, size):
    return min(offset % size, -offset % size)


def halves(x):
    high = x.astype(BF16)
    return high, (x - high.astype(F32)).astype(BF16)


def stacked(x):
    return jnp.concatenate(halves(x), axis=0)


def gram_of(factor):
    return lax.dot_general(factor, factor, (((1,), (1,)), ((), ())), precision=HIGHEST, preferred_element_type=F32)


def packed(gram):
    return jnp.concatenate([gram[:32], gram[32:]], axis=1)


def unpacked(pack):
    return jnp.concatenate([pack[:, :64], pack[:, 64:]], axis=0)


def spread(row, lanes=128):
    return jnp.broadcast_to(row, (8, lanes))


def eliminate(work):
    rows = [work[8 * i : 8 * i + 8] for i in range(8)]
    sublane = lax.broadcasted_iota(jnp.int32, (8, 128), 0)
    for panel in range(8):
        columns = [
            [jnp.broadcast_to(rows[i][:, 8 * panel + k : 8 * panel + k + 1], (8, 128)) for k in range(8)]
            for i in range(8)
        ]
        own = list(columns[panel])
        value = rows[panel]
        inverses = jnp.zeros((8, 128), F32)
        for k in range(8):
            inverse = 1.0 / spread(own[k][k : k + 1])
            inverses = jnp.where(sublane == k, inverse, inverses)
            factor = jnp.where(sublane == k, 0.0, own[k] * inverse)
            value = value - factor * spread(value[k : k + 1])
            for m in range(k + 1, 8):
                own[m] = own[m] - factor * spread(own[m][k : k + 1])
        value = value * inverses
        rows[panel] = value
        pivots = [spread(value[k : k + 1]) for k in range(8)]
        for i in range(8):
            if i != panel:
                total = rows[i]
                for k in range(8):
                    total = total - columns[i][k] * pivots[k]
                rows[i] = total
    return jnp.concatenate(rows, axis=0)[:, 64:]


def kernel(
    tensor, factor_b, factor_c,
    out_a, out_b, out_scales,
    staged, high, low, wide_c, twin_c, gram_c, solved_a, solved_b,
    part_a, sums_a, full_a, grams_a,
    part_b, pair_b, half_b, sums_b, full_b,
    halves_g, pair_g, grams_b, full_g, squares,
    load_sem, send_sem, recv_sem, last_send, last_recv,
):
    row, col = lax.axis_index("row"), lax.axis_index("col")
    chip, core = row // 2, lax.rem(row, 2)
    col_x, col_y = col // SIDE, lax.rem(col, SIDE)
    sibling = (row + 1 - 2 * core, col)

    def at_col(dx, dy):
        return lax.rem(col_x + dx, SIDE), lax.rem(col_y + dy, SIDE)

    def share_of(x, y):
        return lax.rem(x, 2) * SIDE + lax.rem(y + 2 * (x // 2), SIDE)

    def at_chip(offset):
        return lax.rem(chip + offset + CHIPS, CHIPS)

    col_offsets = [(dx, dy) for dx in range(SIDE) for dy in range(SIDE) if (dx, dy) != (0, 0)]
    col_offsets.sort(key=lambda o: -ring(o[0], SIDE) - ring(o[1], SIDE))
    col_peers = [at_col(*offset) for offset in col_offsets]
    chip_offsets = sorted(range(1, CHIPS), key=lambda o: -ring(o, CHIPS))
    chip_peers = [at_chip(offset) for offset in chip_offsets]
    share = share_of(col_x, col_y)
    tile = lax.rem(chip, 8)

    def device_on_col(x, y):
        return (row, x * SIDE + y)

    def device_on_row(z, c):
        return (z * 2 + c, col)

    barrier = pltpu.get_barrier_semaphore()

    chunks = tensor.shape[0]

    def load(k):
        return pltpu.make_async_copy(tensor.at[k], staged.at[k], load_sem.at[k])

    def start_load(k, carry):
        load(k).start()
        return carry

    lax.fori_loop(0, chunks, start_load, 0)

    greeted = [device_on_col(x, y) for x, y in col_peers]
    greeted += [device_on_row(z, c) for z in chip_peers for c in (0, 1)] + [sibling]
    for device in greeted:
        pl.semaphore_signal(barrier, inc=1, device_id=device, device_id_type=MESH)

    c = factor_c[...]
    gram_c[...] = lax.dot_general(c, c, (((0,), (0,)), ((), ())), precision=HIGHEST, preferred_element_type=F32)
    twin_c[...] = jnp.concatenate([c, c], axis=1)
    c_columns = c.T
    for k in range(chunks):
        wide_c[k] = jnp.broadcast_to(c_columns[:, k : k + 1], (64, 128))
    solved_b[...] = factor_b[...]

    def take(k, carry):
        load(k).wait()
        first, second = halves(staged[k])
        high[k] = first
        low[k] = second
        return carry

    lax.fori_loop(0, chunks, take, 0)

    eye = jnp.where(
        lax.broadcasted_iota(jnp.int32, (64, 64), 0) == lax.broadcasted_iota(jnp.int32, (64, 64), 1), 1.0, 0.0
    ).astype(F32)
    rows_all = 32.0 * tensor.shape[1]
    cols_all = 16.0 * tensor.shape[2]

    def scales_row(gram, count):
        return jnp.sqrt(jnp.sum(gram * eye, axis=0, keepdims=True) / count + EPSILON)

    def scales_column(gram, count):
        return jnp.sqrt(jnp.sum(gram * eye, axis=1, keepdims=True) / count + EPSILON)

    def send(source, target, sweep, kind, device):
        pltpu.make_async_remote_copy(
            src_ref=source, dst_ref=target, send_sem=send_sem.at[sweep, kind], recv_sem=recv_sem.at[sweep, kind],
            device_id=device, device_id_type=MESH,
        ).start()

    def arrived(like, sweep, kind):
        pltpu.make_async_copy(like, like, recv_sem.at[sweep, kind]).wait()

    def left(like, sweep, kind):
        pltpu.make_async_copy(like, like, send_sem.at[sweep, kind]).wait()

    def added(ref, sweep):
        total = ref[sweep, 0]
        for source in range(1, 16):
            total = total + ref[sweep, source]
        return total

    pl.semaphore_wait(barrier, len(greeted))

    def sweep_body(sweep, carry):
        b = solved_b[...]
        grams_a[sweep, col] = packed(gram_of(b))
        for x, y in col_peers:
            send(grams_a.at[sweep, col], grams_a.at[sweep, col], sweep, 0, device_on_col(x, y))
        weights = stacked(b)
        total = jnp.zeros((256, 128), F32)
        for k in range(chunks):
            part = lax.dot_general(high[k], weights, (((1,), (1,)), ((), ())), preferred_element_type=F32)
            part = part + lax.dot_general(low[k], weights, (((1,), (1,)), ((), ())), preferred_element_type=F32)
            total = total + part * twin_c[k : k + 1, :]
        part_a[sweep] = (total[:, :64] + total[:, 64:]).T.reshape(8, 8, 256)
        for x, y in col_peers:
            send(part_a.at[sweep, share_of(x, y)], sums_a.at[sweep, col], sweep, 1, device_on_col(x, y))
        sums_a[sweep, col] = part_a[sweep, share]
        arrived(sums_a.at[sweep, pl.ds(0, 15)], sweep, 1)
        full_a[sweep, share] = added(sums_a, sweep)
        for offset in SERVED[1:]:
            send(full_a.at[sweep, share], full_a.at[sweep, share], sweep, 2, device_on_col(*at_col(*offset)))
        arrived(grams_a.at[sweep, pl.ds(0, 15)], sweep, 0)
        gram = unpacked(added(grams_a, sweep))
        given = sweep == 0
        across = jnp.where(given, 1.0, 1.0 / scales_row(gram, cols_all))
        down = jnp.where(given, 1.0, 1.0 / scales_column(gram, cols_all))
        system = gram_c[...] * (gram * down * across) + cols_all * eye
        solver = eliminate(jnp.concatenate([system, eye * across], axis=1))
        arrived(full_a.at[sweep, pl.ds(0, 7)], sweep, 2)
        a = jnp.dot(solver, full_a[sweep].reshape(64, 256), precision=HIGHEST, preferred_element_type=F32)
        solved_a[...] = a

        halves_g[sweep] = packed(gram_of(a)).reshape(2, 16, 128)
        send(halves_g.at[sweep, 1 - core], pair_g.at[sweep], sweep, 3, sibling)
        total = jnp.zeros((128, 256), F32)
        for k in range(chunks):
            scaled = jnp.concatenate([wide_c[k], wide_c[k]], axis=1) * a
            weights = stacked(scaled)
            total = total + jnp.dot(weights, high[k], preferred_element_type=F32)
            total = total + jnp.dot(weights, low[k], preferred_element_type=F32)
        total = total[:64] + total[64:]
        part_b[sweep, 0] = total[:, :128]
        part_b[sweep, 1] = total[:, 128:]
        send(part_b.at[sweep, 1 - core], pair_b.at[sweep], sweep, 4, sibling)
        arrived(pair_g.at[sweep], sweep, 3)
        grams_b[sweep, chip] = halves_g[sweep, core] + pair_g[sweep]
        for z in chip_peers:
            send(grams_b.at[sweep, chip], grams_b.at[sweep, chip], sweep, 5, device_on_row(z, core))
        arrived(pair_b.at[sweep], sweep, 4)
        half_b[sweep] = (part_b[sweep, core] + pair_b[sweep]).reshape(8, 8, 128)
        for z in chip_peers:
            send(half_b.at[sweep, lax.rem(z, 8)], sums_b.at[sweep, chip], sweep, 6, device_on_row(z, core))
        sums_b[sweep, chip] = half_b[sweep, tile]
        arrived(grams_b.at[sweep, pl.ds(0, 15)], sweep, 5)
        full_g[sweep, core] = added(grams_b, sweep)
        send(full_g.at[sweep, core], full_g.at[sweep, core], sweep, 7, sibling)
        arrived(sums_b.at[sweep, pl.ds(0, 15)], sweep, 6)
        full_b[sweep, core, tile] = added(sums_b, sweep)
        for offset in WINDOW:
            z = at_chip(offset)
            own = full_b.at[sweep, core, tile]
            send(own, own, sweep, 8, device_on_row(z, 1 - core))
            if offset:
                send(own, own, sweep, 8, device_on_row(z, core))
        arrived(pair_g.at[sweep], sweep, 7)
        gram = unpacked(full_g[sweep].reshape(32, 128))
        scales = scales_row(gram, rows_all)
        out_scales[0:1, :] = scales
        across = 1.0 / scales
        down = 1.0 / scales_column(gram, rows_all)
        out_a[...] = a * down
        system = gram_c[...] * (gram * down * across) + rows_all * eye
        solver = eliminate(jnp.concatenate([system, eye * across], axis=1))
        arrived(sums_b.at[sweep, pl.ds(0, 15)], sweep, 8)
        summed = jnp.concatenate([full_b[sweep, 0].reshape(64, 128), full_b[sweep, 1].reshape(64, 128)], axis=1)
        solved_b[...] = jnp.dot(solver, summed, precision=HIGHEST, preferred_element_type=F32)
        return carry

    lax.fori_loop(0, SWEEPS, sweep_body, 0)

    b = solved_b[...]
    own = jnp.sum(gram_of(b) * eye, axis=0, keepdims=True)
    squares[col] = jnp.concatenate([own, own], axis=1)
    for x, y in col_peers:
        pltpu.make_async_remote_copy(
            src_ref=squares.at[col], dst_ref=squares.at[col], send_sem=last_send, recv_sem=last_recv,
            device_id=device_on_col(x, y), device_id_type=MESH,
        ).start()
    pltpu.make_async_copy(squares.at[pl.ds(0, 15)], squares.at[pl.ds(0, 15)], last_recv).wait()
    total = squares[0]
    for source in range(1, COLS):
        total = total + squares[source]
    scales = jnp.sqrt(total[:, :64] / cols_all + EPSILON)
    out_scales[1:2, :] = scales
    out_b[...] = b / jnp.sum(eye * scales, axis=1, keepdims=True)

    def drain(sweep, carry):
        left(grams_a.at[sweep, pl.ds(0, 15)], sweep, 0)
        left(sums_a.at[sweep, pl.ds(0, 15)], sweep, 1)
        left(full_a.at[sweep, pl.ds(0, 7)], sweep, 2)
        left(pair_g.at[sweep], sweep, 3)
        left(pair_b.at[sweep], sweep, 4)
        left(grams_b.at[sweep, pl.ds(0, 15)], sweep, 5)
        left(sums_b.at[sweep, pl.ds(0, 15)], sweep, 6)
        left(pair_g.at[sweep], sweep, 7)
        left(sums_b.at[sweep, pl.ds(0, 15)], sweep, 8)
        return carry

    lax.fori_loop(0, SWEEPS, drain, 0)
    pltpu.make_async_copy(squares.at[pl.ds(0, 15)], squares.at[pl.ds(0, 15)], last_send).wait()


def shards(tensor, factor_b, factor_c):
    vmem = pl.BlockSpec(memory_space=pltpu.VMEM)
    whole = pl.BlockSpec(memory_space=pl.ANY)
    n = SWEEPS
    return pl.pallas_call(
        kernel,
        out_shape=(
            jax.ShapeDtypeStruct((64, 256), F32),
            jax.ShapeDtypeStruct((64, 256), F32),
            jax.ShapeDtypeStruct((2, 64), F32),
        ),
        in_specs=[whole, vmem, vmem],
        out_specs=(vmem, vmem, vmem),
        scratch_shapes=[
            pltpu.VMEM((16, 256, 256), F32),
            pltpu.VMEM((16, 256, 256), BF16),
            pltpu.VMEM((16, 256, 256), BF16),
            pltpu.VMEM((16, 64, 128), F32),
            pltpu.VMEM((16, 128), F32),
            pltpu.VMEM((64, 64), F32),
            pltpu.VMEM((64, 256), F32),
            pltpu.VMEM((64, 256), F32),
            pltpu.VMEM((n, 8, 8, 256), F32),
            pltpu.VMEM((n, 16, 8, 256), F32),
            pltpu.VMEM((n, 8, 8, 256), F32),
            pltpu.VMEM((n, 16, 32, 128), F32),
            pltpu.VMEM((n, 2, 64, 128), F32),
            pltpu.VMEM((n, 64, 128), F32),
            pltpu.VMEM((n, 8, 8, 128), F32),
            pltpu.VMEM((n, 16, 8, 128), F32),
            pltpu.VMEM((n, 2, 8, 8, 128), F32),
            pltpu.VMEM((n, 2, 16, 128), F32),
            pltpu.VMEM((n, 16, 128), F32),
            pltpu.VMEM((n, 16, 16, 128), F32),
            pltpu.VMEM((n, 2, 16, 128), F32),
            pltpu.VMEM((16, 1, 128), F32),
            pltpu.SemaphoreType.DMA((16,)),
            pltpu.SemaphoreType.DMA((n, 9)),
            pltpu.SemaphoreType.DMA((n, 9)),
            pltpu.SemaphoreType.DMA,
            pltpu.SemaphoreType.DMA,
        ],
        compiler_params=pltpu.CompilerParams(collective_id=0, has_side_effects=True, vmem_limit_bytes=40 * 2**20),
        name="sweeps",
    )(tensor, factor_b, factor_c)


def solution(mesh):
    in_specs = (P(None, "row", "col"), P(None, "col"), P())
    out_specs = (P(None, "row"), P(None, "col"), P())
    return jax.shard_map(shards, mesh=mesh, in_specs=in_specs, out_specs=out_specs, check_vma=False)
```

```python
import jax
import jax.numpy as jnp
from jax import lax
from jax.experimental import pallas as pl
from jax.experimental.pallas import tpu as pltpu
from jax.sharding import PartitionSpec as P

SWEEPS = 3
EPSILON = 1e-06
MESH = pl.DeviceIdType.MESH
HIGHEST = lax.Precision.HIGHEST
F32 = jnp.float32
BF16 = jnp.bfloat16

CHIPS = 16
COLS = 16
SIDE = 4

SERVED = ((0, 0), (1, 0), (3, 0), (0, 1), (0, 3), (2, 0), (1, 1), (1, 3))
WINDOW = (-4, -3, 3, -2, 2, -1, 1, 0)


def ring(offset, size):
    return min(offset % size, -offset % size)


def halves(x):
    high = x.astype(BF16)
    return high, (x - high.astype(F32)).astype(BF16)


def stacked(x):
    return jnp.concatenate(halves(x), axis=0)


def gram_of(factor):
    return lax.dot_general(factor, factor, (((1,), (1,)), ((), ())), precision=HIGHEST, preferred_element_type=F32)


def packed(gram):
    return jnp.concatenate([gram[:32], gram[32:]], axis=1)


def unpacked(pack):
    return jnp.concatenate([pack[:, :64], pack[:, 64:]], axis=0)


def spread(row, lanes=128):
    return jnp.broadcast_to(row, (8, lanes))


def eliminate(work):
    rows = [work[8 * i : 8 * i + 8] for i in range(8)]
    sublane = lax.broadcasted_iota(jnp.int32, (8, 128), 0)
    for panel in range(8):
        lane = 8 * panel
        value = rows[panel]
        own = [spread(value[:, lane + k : lane + k + 1]) for k in range(8)]
        factors = []
        inverses = jnp.zeros((8, 128), F32)
        for k in range(8):
            inverse = 1.0 / spread(own[k][k : k + 1])
            inverses = jnp.where(sublane == k, inverse, inverses)
            factors.append(jnp.where(sublane == k, 0.0, own[k] * inverse))
            for m in range(k + 1, 8):
                own[m] = own[m] - factors[k] * spread(own[m][k : k + 1])
        for k in range(8):
            value = value - factors[k] * spread(value[k : k + 1])
        value = value * inverses
        rows[panel] = value
        pivots = [spread(value[k : k + 1]) for k in range(8)]
        for i in range(8):
            if i != panel:
                terms = [spread(rows[i][:, lane + k : lane + k + 1]) * pivots[k] for k in range(8)]
                while len(terms) > 1:
                    terms = [x + y for x, y in zip(terms[::2], terms[1::2])]
                rows[i] = rows[i] - terms[0]
    return jnp.concatenate(rows, axis=0)[:, 64:]


def kernel(
    tensor, factor_b, factor_c,
    out_a, out_b, out_scales,
    staged, high, low, high_t, low_t, wide_c, twin_c, gram_c, solved_b,
    part_a, sums_a, full_a, grams_a,
    part_b, pair_b, half_b, sums_b, full_b,
    whole_g, halves_g, pair_g, grams_b, full_g, squares,
    own_c, small_sem, load_sem, send_sem, recv_sem, last_send, last_recv,
):
    row, col = lax.axis_index("row"), lax.axis_index("col")
    chip, core = row // 2, lax.rem(row, 2)
    col_x, col_y = col // SIDE, lax.rem(col, SIDE)
    sibling = (row + 1 - 2 * core, col)

    def at_col(dx, dy):
        return lax.rem(col_x + dx, SIDE), lax.rem(col_y + dy, SIDE)

    def share_of(x, y):
        return lax.rem(x, 2) * SIDE + lax.rem(y + 2 * (x // 2), SIDE)

    def at_chip(offset):
        return lax.rem(chip + offset + CHIPS, CHIPS)

    col_offsets = [(dx, dy) for dx in range(SIDE) for dy in range(SIDE) if (dx, dy) != (0, 0)]
    col_offsets.sort(key=lambda o: -ring(o[0], SIDE) - ring(o[1], SIDE))
    col_peers = [at_col(*offset) for offset in col_offsets]
    chip_offsets = sorted(range(1, CHIPS), key=lambda o: -ring(o, CHIPS))
    chip_peers = [at_chip(offset) for offset in chip_offsets]
    x_peers = [lax.rem(col_x + dx, SIDE) for dx in (2, 1, 3)]
    share = share_of(col_x, col_y)
    tile = lax.rem(chip, 8)

    def device_on_col(x, y):
        return (row, x * SIDE + y)

    def device_on_row(z, c):
        return (z * 2 + c, col)

    def device_across(x, c):
        return (chip * 2 + c, x * SIDE + col_y)

    barrier = pltpu.get_barrier_semaphore()

    chunks = tensor.shape[0]

    def load(k):
        return pltpu.make_async_copy(tensor.at[k], staged.at[k], load_sem.at[k])

    def start_load(k, carry):
        load(k).start()
        return carry

    small = [
        pltpu.make_async_copy(factor_c, own_c, small_sem.at[0]),
        pltpu.make_async_copy(factor_b, solved_b, small_sem.at[1]),
    ]
    for copy in small:
        copy.start()
    lax.fori_loop(0, chunks, start_load, 0)

    greeted = [device_on_col(x, y) for x, y in col_peers]
    greeted += [device_on_row(z, c) for z in chip_peers for c in (0, 1)] + [sibling]
    greeted += [device_across(x, 1 - core) for x in x_peers]
    for device in greeted:
        pl.semaphore_signal(barrier, inc=1, device_id=device, device_id_type=MESH)

    small[0].wait()
    c = own_c[...]
    gram_c[...] = lax.dot_general(c, c, (((0,), (0,)), ((), ())), precision=HIGHEST, preferred_element_type=F32)
    twin_c[...] = jnp.concatenate([c, c], axis=1)
    c_columns = c.T
    for k in range(chunks):
        wide_c[k] = jnp.broadcast_to(c_columns[:, k : k + 1], (64, 128))
    small[1].wait()

    eye = jnp.where(
        lax.broadcasted_iota(jnp.int32, (64, 64), 0) == lax.broadcasted_iota(jnp.int32, (64, 64), 1), 1.0, 0.0
    ).astype(F32)
    rows_all = 32.0 * tensor.shape[1]
    cols_all = 16.0 * tensor.shape[2]

    def scales_row(gram, count):
        return jnp.sqrt(jnp.sum(gram * eye, axis=0, keepdims=True) / count + EPSILON)

    def scales_column(gram, count):
        return jnp.sqrt(jnp.sum(gram * eye, axis=1, keepdims=True) / count + EPSILON)

    def send(source, target, sweep, kind, device):
        pltpu.make_async_remote_copy(
            src_ref=source, dst_ref=target, send_sem=send_sem.at[sweep, kind], recv_sem=recv_sem.at[sweep, kind],
            device_id=device, device_id_type=MESH,
        ).start()

    def arrived(like, sweep, kind):
        pltpu.make_async_copy(like, like, recv_sem.at[sweep, kind]).wait()

    def left(like, sweep, kind):
        pltpu.make_async_copy(like, like, send_sem.at[sweep, kind]).wait()

    def added(ref, sweep):
        total = ref[sweep, 0]
        for source in range(1, 16):
            total = total + ref[sweep, source]
        return total

    def mttkrp(factor, first, second):
        total = jnp.zeros((128, 256), F32)
        for k in range(chunks):
            weights = stacked(jnp.concatenate([wide_c[k], wide_c[k]], axis=1) * factor)
            total = total + jnp.dot(weights, first[k], preferred_element_type=F32)
            total = total + jnp.dot(weights, second[k], preferred_element_type=F32)
        return total[:64] + total[64:]

    def keep_gram_a(sweep, b):
        pack = packed(gram_of(b))
        grams_a[sweep, col] = jnp.where(core == 0, pack[:16], pack[16:])

    b = solved_b[...]
    weights_b = stacked(b)

    def take(group, total):
        for i in range(4):
            load(4 * group + i).wait()
        for i in range(4):
            k = 4 * group + i
            first, second = halves(staged[k])
            high[k] = first
            low[k] = second
            part = lax.dot_general(first, weights_b, (((1,), (1,)), ((), ())), preferred_element_type=F32)
            part = part + lax.dot_general(second, weights_b, (((1,), (1,)), ((), ())), preferred_element_type=F32)
            total = total + part * twin_c[pl.ds(k, 1), :]
        return total

    total = lax.fori_loop(0, chunks // 4, take, jnp.zeros((256, 128), F32))
    part_a[0] = (total[:, :64] + total[:, 64:]).T.reshape(8, 8, 256)
    keep_gram_a(0, b)
    pl.semaphore_wait(barrier, len(greeted))

    def turn(k, carry):
        high_t[k] = high[k].T
        low_t[k] = low[k].T
        return carry

    def sweep_body(sweep, carry):
        for x, y in col_peers:
            send(part_a.at[sweep, share_of(x, y)], sums_a.at[sweep, col], sweep, 1, device_on_col(x, y))
        for x, y in col_peers:
            send(grams_a.at[sweep, col], grams_a.at[sweep, col], sweep, 0, device_on_col(x, y))
        sums_a[sweep, col] = part_a[sweep, share]

        @pl.when(sweep == 0)
        def _():
            lax.fori_loop(0, chunks, turn, 0)

        arrived(sums_a.at[sweep, pl.ds(0, 15)], sweep, 1)
        full_a[sweep, share] = added(sums_a, sweep)
        for offset in SERVED[1:]:
            send(full_a.at[sweep, share], full_a.at[sweep, share], sweep, 2, device_on_col(*at_col(*offset)))
        arrived(grams_a.at[sweep, pl.ds(0, 15)], sweep, 0)
        whole_g[sweep, core] = added(grams_a, sweep)
        send(whole_g.at[sweep, core], whole_g.at[sweep, core], sweep, 9, sibling)
        arrived(whole_g.at[sweep, 0], sweep, 9)
        gram = unpacked(whole_g[sweep].reshape(32, 128))
        given = sweep == 0
        across = jnp.where(given, 1.0, 1.0 / scales_row(gram, cols_all))
        down = jnp.where(given, 1.0, 1.0 / scales_column(gram, cols_all))
        system = gram_c[...] * (gram * down * across) + cols_all * eye
        solver = eliminate(jnp.concatenate([system, eye * across], axis=1))
        arrived(full_a.at[sweep, pl.ds(0, 7)], sweep, 2)
        a = jnp.dot(solver, full_a[sweep].reshape(64, 256), precision=HIGHEST, preferred_element_type=F32)

        pack = packed(gram_of(a))
        for half in range(2):
            for x in range(SIDE):
                at = 16 * half + 4 * x
                halves_g[sweep, half, x] = pack[at : at + 4]
        send(halves_g.at[sweep, 1 - core, col_x], pair_g.at[sweep], sweep, 3, sibling)
        total = mttkrp(a, high, low)
        part_b[sweep, 0] = total[:, :128]
        part_b[sweep, 1] = total[:, 128:]
        send(part_b.at[sweep, 1 - core], pair_b.at[sweep], sweep, 4, sibling)
        arrived(pair_g.at[sweep], sweep, 3)
        grams_b[sweep, chip] = halves_g[sweep, core, col_x] + pair_g[sweep]
        for z in chip_peers:
            send(grams_b.at[sweep, chip], grams_b.at[sweep, chip], sweep, 5, device_on_row(z, core))
        arrived(pair_b.at[sweep], sweep, 4)
        half_b[sweep] = (part_b[sweep, core] + pair_b[sweep]).reshape(8, 8, 128)
        for z in chip_peers:
            send(half_b.at[sweep, lax.rem(z, 8)], sums_b.at[sweep, chip], sweep, 6, device_on_row(z, core))
        sums_b[sweep, chip] = half_b[sweep, tile]
        arrived(grams_b.at[sweep, pl.ds(0, 15)], sweep, 5)
        full_g[sweep, core, col_x] = added(grams_b, sweep)
        piece = full_g.at[sweep, core, col_x]
        for x in x_peers:
            for c in (0, 1):
                send(piece, piece, sweep, 7, device_across(x, c))
        send(piece, piece, sweep, 7, sibling)
        arrived(sums_b.at[sweep, pl.ds(0, 15)], sweep, 6)
        full_b[sweep, core, tile] = added(sums_b, sweep)
        for offset in WINDOW:
            z = at_chip(offset * (1 - 2 * core))
            own = full_b.at[sweep, core, tile]
            send(own, own, sweep, 8, device_on_row(z, 1 - core))
            if offset:
                send(own, own, sweep, 8, device_on_row(z, core))
        arrived(grams_b.at[sweep, pl.ds(0, 7)], sweep, 7)
        gram = unpacked(jnp.concatenate([full_g[sweep, half, x] for half in range(2) for x in range(SIDE)], axis=0))
        scales = scales_row(gram, rows_all)
        out_scales[0:1, :] = scales
        across = 1.0 / scales
        down = 1.0 / scales_column(gram, rows_all)
        out_a[...] = a * down
        system = gram_c[...] * (gram * down * across) + rows_all * eye
        solver = eliminate(jnp.concatenate([system, eye * across], axis=1))
        arrived(sums_b.at[sweep, pl.ds(0, 15)], sweep, 8)
        summed = jnp.concatenate([full_b[sweep, 0].reshape(64, 128), full_b[sweep, 1].reshape(64, 128)], axis=1)

        @pl.when(sweep < SWEEPS - 1)
        def _():
            b = jnp.dot(solver, summed, precision=HIGHEST, preferred_element_type=F32)
            part_a[sweep + 1] = mttkrp(b, high_t, low_t).reshape(8, 8, 256)
            keep_gram_a(sweep + 1, b)

        @pl.when(sweep == SWEEPS - 1)
        def _():
            solved_b[...] = jnp.dot(solver, summed, precision=HIGHEST, preferred_element_type=F32)

        return carry

    lax.fori_loop(0, SWEEPS, sweep_body, 0)

    b = solved_b[...]
    own = jnp.sum(gram_of(b) * eye, axis=0, keepdims=True)
    squares[col] = jnp.concatenate([own, own], axis=1)
    for x, y in col_peers:
        pltpu.make_async_remote_copy(
            src_ref=squares.at[col], dst_ref=squares.at[col], send_sem=last_send, recv_sem=last_recv,
            device_id=device_on_col(x, y), device_id_type=MESH,
        ).start()
    pltpu.make_async_copy(squares.at[pl.ds(0, 15)], squares.at[pl.ds(0, 15)], last_recv).wait()
    total = squares[0]
    for source in range(1, COLS):
        total = total + squares[source]
    scales = jnp.sqrt(total[:, :64] / cols_all + EPSILON)
    out_scales[1:2, :] = scales
    out_b[...] = b / jnp.sum(eye * scales, axis=1, keepdims=True)

    def drain(sweep, carry):
        left(grams_a.at[sweep, pl.ds(0, 15)], sweep, 0)
        left(sums_a.at[sweep, pl.ds(0, 15)], sweep, 1)
        left(full_a.at[sweep, pl.ds(0, 7)], sweep, 2)
        left(pair_g.at[sweep], sweep, 3)
        left(pair_b.at[sweep], sweep, 4)
        left(grams_b.at[sweep, pl.ds(0, 15)], sweep, 5)
        left(sums_b.at[sweep, pl.ds(0, 15)], sweep, 6)
        left(grams_b.at[sweep, pl.ds(0, 7)], sweep, 7)
        left(sums_b.at[sweep, pl.ds(0, 15)], sweep, 8)
        left(whole_g.at[sweep, 0], sweep, 9)
        return carry

    lax.fori_loop(0, SWEEPS, drain, 0)
    pltpu.make_async_copy(squares.at[pl.ds(0, 15)], squares.at[pl.ds(0, 15)], last_send).wait()


def place(a, b, scales, out_a, out_b, out_scales):
    out_a[...] = a[...]
    out_b[...] = b[...]
    out_scales[...] = scales[...]


def shards(tensor, factor_b, factor_c):
    vmem = pl.BlockSpec(memory_space=pltpu.VMEM)
    whole = pl.BlockSpec(memory_space=pl.ANY)
    n = SWEEPS
    outs = (
        jax.ShapeDtypeStruct((64, 256), F32),
        jax.ShapeDtypeStruct((64, 256), F32),
        jax.ShapeDtypeStruct((2, 64), F32),
    )
    results = pl.pallas_call(
        kernel,
        out_shape=outs,
        in_specs=[whole, whole, whole],
        out_specs=(vmem, vmem, vmem),
        scratch_shapes=[
            pltpu.VMEM((16, 256, 256), F32),
            pltpu.VMEM((16, 256, 256), BF16),
            pltpu.VMEM((16, 256, 256), BF16),
            pltpu.VMEM((16, 256, 256), BF16),
            pltpu.VMEM((16, 256, 256), BF16),
            pltpu.VMEM((16, 64, 128), F32),
            pltpu.VMEM((16, 128), F32),
            pltpu.VMEM((64, 64), F32),
            pltpu.VMEM((64, 256), F32),
            pltpu.VMEM((n, 8, 8, 256), F32),
            pltpu.VMEM((n, 16, 8, 256), F32),
            pltpu.VMEM((n, 8, 8, 256), F32),
            pltpu.VMEM((n, 16, 16, 128), F32),
            pltpu.VMEM((n, 2, 64, 128), F32),
            pltpu.VMEM((n, 64, 128), F32),
            pltpu.VMEM((n, 8, 8, 128), F32),
            pltpu.VMEM((n, 16, 8, 128), F32),
            pltpu.VMEM((n, 2, 8, 8, 128), F32),
            pltpu.VMEM((n, 2, 16, 128), F32),
            pltpu.VMEM((n, 2, 4, 4, 128), F32),
            pltpu.VMEM((n, 4, 128), F32),
            pltpu.VMEM((n, 16, 4, 128), F32),
            pltpu.VMEM((n, 2, 4, 4, 128), F32),
            pltpu.VMEM((16, 1, 128), F32),
            pltpu.VMEM((16, 64), F32),
            pltpu.SemaphoreType.DMA((2,)),
            pltpu.SemaphoreType.DMA((16,)),
            pltpu.SemaphoreType.DMA((n, 10)),
            pltpu.SemaphoreType.DMA((n, 10)),
            pltpu.SemaphoreType.DMA,
            pltpu.SemaphoreType.DMA,
        ],
        compiler_params=pltpu.CompilerParams(collective_id=0, has_side_effects=True, vmem_limit_bytes=54 * 2**20),
        name="sweeps",
    )(tensor, factor_b, factor_c)
    return pl.pallas_call(
        place,
        out_shape=outs,
        in_specs=[vmem] * 3,
        out_specs=(vmem, vmem, vmem),
        compiler_params=pltpu.CompilerParams(vmem_limit_bytes=54 * 2**20),
        name="place",
    )(*results)


def solution(mesh):
    in_specs = (P(None, "row", "col"), P(None, "col"), P())
    out_specs = (P(None, "row"), P(None, "col"), P())
    return jax.shard_map(shards, mesh=mesh, in_specs=in_specs, out_specs=out_specs, check_vma=False)
```

```python
import jax
import jax.numpy as jnp
from jax import lax
from jax.experimental import pallas as pl
from jax.experimental.pallas import tpu as pltpu
from jax.sharding import PartitionSpec as P

SWEEPS = 3
EPSILON = 1e-06
MESH = pl.DeviceIdType.MESH
HIGHEST = lax.Precision.HIGHEST
F32 = jnp.float32
BF16 = jnp.bfloat16

CHIPS = 16
COLS = 16
SIDE = 4

WINDOW = (-4, -3, 3, -2, 2, -1, 1, 0)


def ring(offset, size):
    return min(offset % size, -offset % size)


def halves(x):
    high = x.astype(BF16)
    return high, (x - high.astype(F32)).astype(BF16)


def stacked(x):
    return jnp.concatenate(halves(x), axis=0)


def gram_of(factor):
    return lax.dot_general(factor, factor, (((1,), (1,)), ((), ())), precision=HIGHEST, preferred_element_type=F32)


def packed(gram):
    return jnp.concatenate([gram[:32], gram[32:]], axis=1)


def unpacked(pack):
    return jnp.concatenate([pack[:, :64], pack[:, 64:]], axis=0)


def spread(row, lanes=128):
    return jnp.broadcast_to(row, (8, lanes))


def eliminate(work):
    rows = [work[8 * i : 8 * i + 8] for i in range(8)]
    sublane = lax.broadcasted_iota(jnp.int32, (8, 128), 0)
    for panel in range(8):
        lane = 8 * panel
        value = rows[panel]
        own = [spread(value[:, lane + k : lane + k + 1]) for k in range(8)]
        factors = []
        inverses = jnp.zeros((8, 128), F32)
        for k in range(8):
            inverse = 1.0 / spread(own[k][k : k + 1])
            inverses = jnp.where(sublane == k, inverse, inverses)
            factors.append(jnp.where(sublane == k, 0.0, own[k] * inverse))
            for m in range(k + 1, 8):
                own[m] = own[m] - factors[k] * spread(own[m][k : k + 1])
        for k in range(8):
            value = value - factors[k] * spread(value[k : k + 1])
        value = value * inverses
        rows[panel] = value
        pivots = [spread(value[k : k + 1]) for k in range(8)]
        for i in range(8):
            if i != panel:
                terms = [spread(rows[i][:, lane + k : lane + k + 1]) * pivots[k] for k in range(8)]
                while len(terms) > 1:
                    terms = [x + y for x, y in zip(terms[::2], terms[1::2])]
                rows[i] = rows[i] - terms[0]
    return jnp.concatenate(rows, axis=0)[:, 64:]


def kernel(
    tensor, factor_b, factor_c,
    out_a, out_b, out_scales,
    staged, high, low, high_t, low_t, wide_c, twin_c, gram_c, solved_b,
    part_a, sums_a, full_a, grams_a,
    part_b, pair_b, half_b, sums_b, full_b,
    whole_g, pieces_g, grams_b, full_g, squares,
    own_c, small_sem, load_sem, send_sem, recv_sem, last_send, last_recv,
):
    row, col = lax.axis_index("row"), lax.axis_index("col")
    chip, core = row // 2, lax.rem(row, 2)
    col_x, col_y = col // SIDE, lax.rem(col, SIDE)
    sibling = (row + 1 - 2 * core, col)

    def at_col(dx, dy):
        return lax.rem(col_x + dx, SIDE), lax.rem(col_y + dy, SIDE)

    def at_chip(offset):
        return lax.rem(chip + offset + CHIPS, CHIPS)

    col_offsets = [(dx, dy) for dx in range(SIDE) for dy in range(SIDE) if (dx, dy) != (0, 0)]
    col_offsets.sort(key=lambda o: -ring(o[0], SIDE) - ring(o[1], SIDE))
    col_peers = [at_col(*offset) for offset in col_offsets]
    chip_offsets = sorted(range(1, CHIPS), key=lambda o: -ring(o, CHIPS))
    chip_peers = [at_chip(offset) for offset in chip_offsets]
    tile = lax.rem(chip, 8)

    def device_on_col(x, y):
        return (row, x * SIDE + y)

    def device_on_row(z, c):
        return (z * 2 + c, col)

    def device_across(x, y, c):
        return (chip * 2 + c, x * SIDE + y)

    barrier = pltpu.get_barrier_semaphore()
    greeted = [device_on_row(z, core) for z in chip_peers]
    greeted += [device_on_row(at_chip(offset * (1 - 2 * core)), 1 - core) for offset in WINDOW]
    greeted += [device_on_col(x, y) for x, y in col_peers]
    greeted += [device_across(x, y, 1 - core) for x, y in col_peers]
    for device in greeted[:15]:
        pl.semaphore_signal(barrier, inc=1, device_id=device, device_id_type=MESH)

    chunks = tensor.shape[0]

    def load(k):
        return pltpu.make_async_copy(tensor.at[k], staged.at[k], load_sem.at[k])

    def start_load(k, carry):
        load(k).start()
        return carry

    small = [
        pltpu.make_async_copy(factor_c, own_c, small_sem.at[0]),
        pltpu.make_async_copy(factor_b, solved_b, small_sem.at[1]),
    ]
    for copy in small:
        copy.start()
    lax.fori_loop(0, chunks, start_load, 0)
    for device in greeted[15:]:
        pl.semaphore_signal(barrier, inc=1, device_id=device, device_id_type=MESH)

    small[0].wait()
    c = own_c[...]
    gram_c[...] = lax.dot_general(c, c, (((0,), (0,)), ((), ())), precision=HIGHEST, preferred_element_type=F32)
    twin_c[...] = jnp.concatenate([c, c], axis=1)
    c_columns = c.T
    for k in range(chunks):
        wide_c[k] = jnp.broadcast_to(c_columns[:, k : k + 1], (64, 128))
    small[1].wait()

    eye = jnp.where(
        lax.broadcasted_iota(jnp.int32, (64, 64), 0) == lax.broadcasted_iota(jnp.int32, (64, 64), 1), 1.0, 0.0
    ).astype(F32)
    rows_all = 32.0 * tensor.shape[1]
    cols_all = 16.0 * tensor.shape[2]

    def scales_row(gram, count):
        return jnp.sqrt(jnp.sum(gram * eye, axis=0, keepdims=True) / count + EPSILON)

    def scales_column(gram, count):
        return jnp.sqrt(jnp.sum(gram * eye, axis=1, keepdims=True) / count + EPSILON)

    def send(source, target, sweep, kind, device):
        pltpu.make_async_remote_copy(
            src_ref=source, dst_ref=target, send_sem=send_sem.at[sweep, kind], recv_sem=recv_sem.at[sweep, kind],
            device_id=device, device_id_type=MESH,
        ).start()

    def arrived(like, sweep, kind):
        pltpu.make_async_copy(like, like, recv_sem.at[sweep, kind]).wait()

    def left(like, sweep, kind):
        pltpu.make_async_copy(like, like, send_sem.at[sweep, kind]).wait()

    def added(ref, sweep):
        total = ref[sweep, 0]
        for source in range(1, 16):
            total = total + ref[sweep, source]
        return total

    def mttkrp(factor, first, second):
        total = jnp.zeros((128, 256), F32)
        for k in range(chunks):
            weights = stacked(jnp.concatenate([wide_c[k], wide_c[k]], axis=1) * factor)
            total = total + jnp.dot(weights, first[k], preferred_element_type=F32)
            total = total + jnp.dot(weights, second[k], preferred_element_type=F32)
        return total[:64] + total[64:]

    def keep_part_a(sweep, part):
        part_a[sweep, 0:8] = part[:, :128].reshape(8, 8, 128)
        part_a[sweep, 8:16] = part[:, 128:].reshape(8, 8, 128)

    def keep_gram_a(sweep, b):
        pack = packed(gram_of(b))
        grams_a[sweep, col] = jnp.where(core == 0, pack[:16], pack[16:])

    b = solved_b[...]
    weights_b = stacked(b)

    def take(group, total):
        for i in range(4):
            load(4 * group + i).wait()
        for i in range(4):
            k = 4 * group + i
            first, second = halves(staged[k])
            high[k] = first
            low[k] = second
            part = lax.dot_general(first, weights_b, (((1,), (1,)), ((), ())), preferred_element_type=F32)
            part = part + lax.dot_general(second, weights_b, (((1,), (1,)), ((), ())), preferred_element_type=F32)
            total = total + part * twin_c[pl.ds(k, 1), :]
        return total

    total = lax.fori_loop(0, chunks // 4, take, jnp.zeros((256, 128), F32))
    keep_part_a(0, (total[:, :64] + total[:, 64:]).T)
    keep_gram_a(0, b)
    pl.semaphore_wait(barrier, len(greeted))

    def turn(k, carry):
        high_t[k] = high[k].T
        low_t[k] = low[k].T
        return carry

    def sweep_body(sweep, carry):
        for x, y in col_peers:
            send(part_a.at[sweep, x * SIDE + y], sums_a.at[sweep, col], sweep, 1, device_on_col(x, y))
        for x, y in col_peers:
            send(grams_a.at[sweep, col], grams_a.at[sweep, col], sweep, 0, device_on_col(x, y))
        sums_a[sweep, col] = part_a[sweep, col]

        @pl.when(sweep == 0)
        def _():
            lax.fori_loop(0, chunks, turn, 0)

        arrived(sums_a.at[sweep, pl.ds(0, 15)], sweep, 1)
        full_a[sweep, col] = added(sums_a, sweep)
        for x, y in col_peers:
            send(full_a.at[sweep, col], full_a.at[sweep, col], sweep, 2, device_on_col(x, y))
        arrived(grams_a.at[sweep, pl.ds(0, 15)], sweep, 0)
        whole_g[sweep, core] = added(grams_a, sweep)
        send(whole_g.at[sweep, core], whole_g.at[sweep, core], sweep, 9, sibling)
        arrived(whole_g.at[sweep, 0], sweep, 9)
        gram = unpacked(whole_g[sweep].reshape(32, 128))
        given = sweep == 0
        across = jnp.where(given, 1.0, 1.0 / scales_row(gram, cols_all))
        down = jnp.where(given, 1.0, 1.0 / scales_column(gram, cols_all))
        system = gram_c[...] * (gram * down * across) + cols_all * eye
        solver = eliminate(jnp.concatenate([system, eye * across], axis=1))
        arrived(full_a.at[sweep, pl.ds(0, 15)], sweep, 2)
        summed = jnp.concatenate([full_a[sweep, 0:8].reshape(64, 128), full_a[sweep, 8:16].reshape(64, 128)], axis=1)
        a = jnp.dot(solver, summed, precision=HIGHEST, preferred_element_type=F32)

        pack = packed(gram_of(a))
        for i in range(COLS):
            pieces_g[sweep, i] = pack[2 * i : 2 * i + 2]
        grams_b[sweep, chip] = pieces_g[sweep, col]
        for z in chip_peers:
            send(grams_b.at[sweep, chip], grams_b.at[sweep, chip], sweep, 5, device_on_row(z, core))
        total = mttkrp(a, high, low)
        part_b[sweep, 0] = total[:, :128]
        part_b[sweep, 1] = total[:, 128:]
        send(part_b.at[sweep, 1 - core], pair_b.at[sweep], sweep, 4, sibling)
        arrived(pair_b.at[sweep], sweep, 4)
        half_b[sweep] = (part_b[sweep, core] + pair_b[sweep]).reshape(8, 8, 128)
        for z in chip_peers:
            send(half_b.at[sweep, lax.rem(z, 8)], sums_b.at[sweep, chip], sweep, 6, device_on_row(z, core))
        sums_b[sweep, chip] = half_b[sweep, tile]
        arrived(grams_b.at[sweep, pl.ds(0, 15)], sweep, 5)
        full_g[sweep, core * COLS + col] = added(grams_b, sweep)
        piece = full_g.at[sweep, core * COLS + col]
        for x, y in col_peers:
            for c in (0, 1):
                send(piece, piece, sweep, 7, device_across(x, y, c))
        send(piece, piece, sweep, 7, sibling)
        arrived(sums_b.at[sweep, pl.ds(0, 15)], sweep, 6)
        full_b[sweep, core, tile] = added(sums_b, sweep)
        for offset in WINDOW:
            z = at_chip(offset * (1 - 2 * core))
            own = full_b.at[sweep, core, tile]
            send(own, own, sweep, 8, device_on_row(z, 1 - core))
            if offset:
                send(own, own, sweep, 8, device_on_row(z, core))
        arrived(full_g.at[sweep, pl.ds(0, 31)], sweep, 7)
        pack = jnp.concatenate([full_g[sweep, i] + full_g[sweep, COLS + i] for i in range(COLS)], axis=0)
        gram = unpacked(pack)
        scales = scales_row(gram, rows_all)
        across = 1.0 / scales
        down = 1.0 / scales_column(gram, rows_all)

        @pl.when(sweep == SWEEPS - 1)
        def _():
            out_scales[0:1, :] = scales
            out_a[...] = a * down

        system = gram_c[...] * (gram * down * across) + rows_all * eye
        solver = eliminate(jnp.concatenate([system, eye * across], axis=1))
        arrived(sums_b.at[sweep, pl.ds(0, 15)], sweep, 8)
        summed = jnp.concatenate([full_b[sweep, 0].reshape(64, 128), full_b[sweep, 1].reshape(64, 128)], axis=1)

        @pl.when(sweep < SWEEPS - 1)
        def _():
            b = jnp.dot(solver, summed, precision=HIGHEST, preferred_element_type=F32)
            keep_part_a(sweep + 1, mttkrp(b, high_t, low_t))
            keep_gram_a(sweep + 1, b)

        @pl.when(sweep == SWEEPS - 1)
        def _():
            solved_b[...] = jnp.dot(solver, summed, precision=HIGHEST, preferred_element_type=F32)

        return carry

    lax.fori_loop(0, SWEEPS, sweep_body, 0)

    b = solved_b[...]
    own = jnp.sum(gram_of(b) * eye, axis=0, keepdims=True)
    squares[col] = jnp.concatenate([own, own], axis=1)
    for x, y in col_peers:
        pltpu.make_async_remote_copy(
            src_ref=squares.at[col], dst_ref=squares.at[col], send_sem=last_send, recv_sem=last_recv,
            device_id=device_on_col(x, y), device_id_type=MESH,
        ).start()
    pltpu.make_async_copy(squares.at[pl.ds(0, 15)], squares.at[pl.ds(0, 15)], last_recv).wait()
    total = squares[0]
    for source in range(1, COLS):
        total = total + squares[source]
    scales = jnp.sqrt(total[:, :64] / cols_all + EPSILON)
    out_scales[1:2, :] = scales
    out_b[...] = b / jnp.sum(eye * scales, axis=1, keepdims=True)

    def drain(sweep, carry):
        left(grams_a.at[sweep, pl.ds(0, 15)], sweep, 0)
        left(sums_a.at[sweep, pl.ds(0, 15)], sweep, 1)
        left(full_a.at[sweep, pl.ds(0, 15)], sweep, 2)
        left(pair_b.at[sweep], sweep, 4)
        left(grams_b.at[sweep, pl.ds(0, 15)], sweep, 5)
        left(sums_b.at[sweep, pl.ds(0, 15)], sweep, 6)
        left(full_g.at[sweep, pl.ds(0, 31)], sweep, 7)
        left(sums_b.at[sweep, pl.ds(0, 15)], sweep, 8)
        left(whole_g.at[sweep, 0], sweep, 9)
        return carry

    lax.fori_loop(0, SWEEPS, drain, 0)
    pltpu.make_async_copy(squares.at[pl.ds(0, 15)], squares.at[pl.ds(0, 15)], last_send).wait()


def place(a, b, scales, out_a, out_b, out_scales):
    out_a[...] = a[...]
    out_b[...] = b[...]
    out_scales[...] = scales[...]


def shards(tensor, factor_b, factor_c):
    vmem = pl.BlockSpec(memory_space=pltpu.VMEM)
    whole = pl.BlockSpec(memory_space=pl.ANY)
    n = SWEEPS
    outs = (
        jax.ShapeDtypeStruct((64, 256), F32),
        jax.ShapeDtypeStruct((64, 256), F32),
        jax.ShapeDtypeStruct((2, 64), F32),
    )
    results = pl.pallas_call(
        kernel,
        out_shape=outs,
        in_specs=[whole, whole, whole],
        out_specs=(vmem, vmem, vmem),
        scratch_shapes=[
            pltpu.VMEM((16, 256, 256), F32),
            pltpu.VMEM((16, 256, 256), BF16),
            pltpu.VMEM((16, 256, 256), BF16),
            pltpu.VMEM((16, 256, 256), BF16),
            pltpu.VMEM((16, 256, 256), BF16),
            pltpu.VMEM((16, 64, 128), F32),
            pltpu.VMEM((16, 128), F32),
            pltpu.VMEM((64, 64), F32),
            pltpu.VMEM((64, 256), F32),
            pltpu.VMEM((n, 16, 8, 128), F32),
            pltpu.VMEM((n, 16, 8, 128), F32),
            pltpu.VMEM((n, 16, 8, 128), F32),
            pltpu.VMEM((n, 16, 16, 128), F32),
            pltpu.VMEM((n, 2, 64, 128), F32),
            pltpu.VMEM((n, 64, 128), F32),
            pltpu.VMEM((n, 8, 8, 128), F32),
            pltpu.VMEM((n, 16, 8, 128), F32),
            pltpu.VMEM((n, 2, 8, 8, 128), F32),
            pltpu.VMEM((n, 2, 16, 128), F32),
            pltpu.VMEM((n, 16, 2, 128), F32),
            pltpu.VMEM((n, 16, 2, 128), F32),
            pltpu.VMEM((n, 32, 2, 128), F32),
            pltpu.VMEM((16, 1, 128), F32),
            pltpu.VMEM((16, 64), F32),
            pltpu.SemaphoreType.DMA((2,)),
            pltpu.SemaphoreType.DMA((16,)),
            pltpu.SemaphoreType.DMA((n, 10)),
            pltpu.SemaphoreType.DMA((n, 10)),
            pltpu.SemaphoreType.DMA,
            pltpu.SemaphoreType.DMA,
        ],
        compiler_params=pltpu.CompilerParams(collective_id=0, has_side_effects=True, vmem_limit_bytes=54 * 2**20),
        name="sweeps",
    )(tensor, factor_b, factor_c)
    return pl.pallas_call(
        place,
        out_shape=outs,
        in_specs=[vmem] * 3,
        out_specs=(vmem, vmem, vmem),
        compiler_params=pltpu.CompilerParams(vmem_limit_bytes=54 * 2**20),
        name="place",
    )(*results)


def solution(mesh):
    in_specs = (P(None, "row", "col"), P(None, "col"), P())
    out_specs = (P(None, "row"), P(None, "col"), P())
    return jax.shard_map(shards, mesh=mesh, in_specs=in_specs, out_specs=out_specs, check_vma=False)
```

```python
import jax
import jax.numpy as jnp
from jax import lax
from jax.experimental import pallas as pl
from jax.experimental.pallas import tpu as pltpu
from jax.sharding import PartitionSpec as P

SWEEPS = 3
EPSILON = 1e-06
MESH = pl.DeviceIdType.MESH
HIGHEST = lax.Precision.HIGHEST
F32 = jnp.float32
BF16 = jnp.bfloat16

CHIPS = 16
COLS = 16
SIDE = 4

WINDOW = (-4, -3, 3, -2, 2, -1, 1, 0)


def ring(offset, size):
    return min(offset % size, -offset % size)


def halves(x):
    high = x.astype(BF16)
    return high, (x - high.astype(F32)).astype(BF16)


def stacked(x):
    return jnp.concatenate(halves(x), axis=0)


def gram_of(factor):
    return lax.dot_general(factor, factor, (((1,), (1,)), ((), ())), precision=HIGHEST, preferred_element_type=F32)


def packed(gram):
    return jnp.concatenate([gram[:32], gram[32:]], axis=1)


def unpacked(pack):
    return jnp.concatenate([pack[:, :64], pack[:, 64:]], axis=0)


def spread(row, lanes=128):
    return jnp.broadcast_to(row, (8, lanes))


def eliminate(work):
    rows = [work[8 * i : 8 * i + 8] for i in range(8)]
    sublane = lax.broadcasted_iota(jnp.int32, (8, 128), 0)
    for panel in range(8):
        lane = 8 * panel
        value = rows[panel]
        own = [spread(value[:, lane + k : lane + k + 1]) for k in range(8)]
        blocks = []
        for k in range(0, 8, 2):
            first, second = own[k], own[k + 1]
            p, q = spread(first[k : k + 1]), spread(second[k : k + 1])
            r, s = spread(first[k + 1 : k + 2]), spread(second[k + 1 : k + 2])
            inverse = 1.0 / (p * s - q * r)
            upper, lower = sublane == k, sublane == k + 1
            one = jnp.where(upper, -s, jnp.where(lower, r, first * s - second * r)) * inverse
            two = jnp.where(upper, q, jnp.where(lower, -p, second * p - first * q)) * inverse
            keep = jnp.where(upper | lower, 0.0, 1.0)
            blocks.append((one, two, keep))
            for m in range(k + 2, 8):
                own[m] = own[m] * keep - one * spread(own[m][k : k + 1]) - two * spread(own[m][k + 1 : k + 2])
        for k, (one, two, keep) in zip(range(0, 8, 2), blocks):
            value = value * keep - one * spread(value[k : k + 1]) - two * spread(value[k + 1 : k + 2])
        rows[panel] = value
        pivots = [spread(value[k : k + 1]) for k in range(8)]
        for i in range(8):
            if i != panel:
                terms = [spread(rows[i][:, lane + k : lane + k + 1]) * pivots[k] for k in range(8)]
                while len(terms) > 1:
                    terms = [x + y for x, y in zip(terms[::2], terms[1::2])]
                rows[i] = rows[i] - terms[0]
    return jnp.concatenate(rows, axis=0)[:, 64:]


def kernel(
    tensor, factor_b, factor_c,
    out_a, out_b, out_scales,
    staged, high, low, high_t, low_t, wide_c, twin_c, gram_c, solved_b,
    part_a, sums_a, full_a, grams_a,
    part_b, pair_b, half_b, sums_b, full_b,
    whole_g, pieces_g, grams_b, full_g, squares,
    own_c, small_sem, load_sem, send_sem, recv_sem, last_send, last_recv,
):
    row, col = lax.axis_index("row"), lax.axis_index("col")
    chip, core = row // 2, lax.rem(row, 2)
    col_x, col_y = col // SIDE, lax.rem(col, SIDE)
    sibling = (row + 1 - 2 * core, col)

    def at_col(dx, dy):
        return lax.rem(col_x + dx, SIDE), lax.rem(col_y + dy, SIDE)

    def at_chip(offset):
        return lax.rem(chip + offset + CHIPS, CHIPS)

    col_offsets = [(dx, dy) for dx in range(SIDE) for dy in range(SIDE) if (dx, dy) != (0, 0)]
    col_offsets.sort(key=lambda o: -ring(o[0], SIDE) - ring(o[1], SIDE))
    col_peers = [at_col(*offset) for offset in col_offsets]
    chip_offsets = sorted(range(1, CHIPS), key=lambda o: -ring(o, CHIPS))
    chip_peers = [at_chip(offset * (1 - 2 * core)) for offset in chip_offsets]
    tile = lax.rem(chip, 8)

    def device_on_col(x, y):
        return (row, x * SIDE + y)

    def device_on_row(z, c):
        return (z * 2 + c, col)

    def device_across(x, y, c):
        return (chip * 2 + c, x * SIDE + y)

    barrier = pltpu.get_barrier_semaphore()
    greeted = [device_on_row(z, core) for z in chip_peers]
    greeted += [device_on_row(at_chip(offset * (1 - 2 * core)), 1 - core) for offset in WINDOW]
    greeted += [device_on_col(x, y) for x, y in col_peers]
    greeted += [device_across(x, y, 1 - core) for x, y in col_peers]
    for device in greeted[:15]:
        pl.semaphore_signal(barrier, inc=1, device_id=device, device_id_type=MESH)

    chunks = tensor.shape[0]

    def load(k):
        return pltpu.make_async_copy(tensor.at[k], staged.at[k], load_sem.at[k])

    def start_load(k, carry):
        load(k).start()
        return carry

    small = [
        pltpu.make_async_copy(factor_c, own_c, small_sem.at[0]),
        pltpu.make_async_copy(factor_b, solved_b, small_sem.at[1]),
    ]
    for copy in small:
        copy.start()
    lax.fori_loop(0, chunks, start_load, 0)
    for device in greeted[15:]:
        pl.semaphore_signal(barrier, inc=1, device_id=device, device_id_type=MESH)

    small[0].wait()
    c = own_c[...]
    gram_c[...] = lax.dot_general(c, c, (((0,), (0,)), ((), ())), precision=HIGHEST, preferred_element_type=F32)
    twin_c[...] = jnp.concatenate([c, c], axis=1)
    c_columns = c.T
    for k in range(chunks):
        wide_c[k] = jnp.broadcast_to(c_columns[:, k : k + 1], (64, 128))
    small[1].wait()

    eye = jnp.where(
        lax.broadcasted_iota(jnp.int32, (64, 64), 0) == lax.broadcasted_iota(jnp.int32, (64, 64), 1), 1.0, 0.0
    ).astype(F32)
    rows_all = 32.0 * tensor.shape[1]
    cols_all = 16.0 * tensor.shape[2]

    def scales_row(gram, count):
        return jnp.sqrt(jnp.sum(gram * eye, axis=0, keepdims=True) / count + EPSILON)

    def scales_column(gram, count):
        return jnp.sqrt(jnp.sum(gram * eye, axis=1, keepdims=True) / count + EPSILON)

    def send(source, target, sweep, kind, device):
        pltpu.make_async_remote_copy(
            src_ref=source, dst_ref=target, send_sem=send_sem.at[sweep, kind], recv_sem=recv_sem.at[sweep, kind],
            device_id=device, device_id_type=MESH,
        ).start()

    def arrived(like, sweep, kind):
        pltpu.make_async_copy(like, like, recv_sem.at[sweep, kind]).wait()

    def left(like, sweep, kind):
        pltpu.make_async_copy(like, like, send_sem.at[sweep, kind]).wait()

    def added(ref, sweep):
        total = ref[sweep, 0]
        for source in range(1, 16):
            total = total + ref[sweep, source]
        return total

    def mttkrp(factor, first, second):
        total = jnp.zeros((128, 256), F32)
        for k in range(chunks):
            weights = stacked(jnp.concatenate([wide_c[k], wide_c[k]], axis=1) * factor)
            total = total + jnp.dot(weights, first[k], preferred_element_type=F32)
            total = total + jnp.dot(weights, second[k], preferred_element_type=F32)
        return total[:64] + total[64:]

    def keep_part_a(sweep, part):
        part_a[sweep, 0:8] = part[:, :128].reshape(8, 8, 128)
        part_a[sweep, 8:16] = part[:, 128:].reshape(8, 8, 128)

    def keep_gram_a(sweep, b):
        pack = packed(gram_of(b))
        grams_a[sweep, col] = jnp.where(core == 0, pack[:16], pack[16:])

    b = solved_b[...]
    weights_b = stacked(b)

    def take(group, total):
        for i in range(4):
            load(4 * group + i).wait()
        for i in range(4):
            k = 4 * group + i
            first, second = halves(staged[k])
            high[k] = first
            low[k] = second
            part = lax.dot_general(first, weights_b, (((1,), (1,)), ((), ())), preferred_element_type=F32)
            part = part + lax.dot_general(second, weights_b, (((1,), (1,)), ((), ())), preferred_element_type=F32)
            total = total + part * twin_c[pl.ds(k, 1), :]
        return total

    total = lax.fori_loop(0, chunks // 4, take, jnp.zeros((256, 128), F32))
    keep_part_a(0, (total[:, :64] + total[:, 64:]).T)
    keep_gram_a(0, b)
    pl.semaphore_wait(barrier, len(greeted))

    def turn(k, carry):
        high_t[k] = high[k].T
        low_t[k] = low[k].T
        return carry

    def sweep_body(sweep, carry):
        for x, y in col_peers:
            send(part_a.at[sweep, x * SIDE + y], sums_a.at[sweep, col], sweep, 1, device_on_col(x, y))
        for x, y in col_peers:
            send(grams_a.at[sweep, col], grams_a.at[sweep, col], sweep, 0, device_on_col(x, y))
        sums_a[sweep, col] = part_a[sweep, col]

        @pl.when(sweep == 0)
        def _():
            lax.fori_loop(0, chunks, turn, 0)

        arrived(sums_a.at[sweep, pl.ds(0, 15)], sweep, 1)
        full_a[sweep, col] = added(sums_a, sweep)
        for x, y in col_peers:
            send(full_a.at[sweep, col], full_a.at[sweep, col], sweep, 2, device_on_col(x, y))
        arrived(grams_a.at[sweep, pl.ds(0, 15)], sweep, 0)
        whole_g[sweep, core] = added(grams_a, sweep)
        send(whole_g.at[sweep, core], whole_g.at[sweep, core], sweep, 9, sibling)
        arrived(whole_g.at[sweep, 0], sweep, 9)
        gram = unpacked(whole_g[sweep].reshape(32, 128))
        given = sweep == 0
        across = jnp.where(given, 1.0, 1.0 / scales_row(gram, cols_all))
        down = jnp.where(given, 1.0, 1.0 / scales_column(gram, cols_all))
        system = gram_c[...] * (gram * down * across) + cols_all * eye
        solver = eliminate(jnp.concatenate([system, eye * across], axis=1))
        arrived(full_a.at[sweep, pl.ds(0, 15)], sweep, 2)
        summed = jnp.concatenate([full_a[sweep, 0:8].reshape(64, 128), full_a[sweep, 8:16].reshape(64, 128)], axis=1)
        a = jnp.dot(solver, summed, precision=HIGHEST, preferred_element_type=F32)

        pack = packed(gram_of(a))
        for i in range(COLS):
            pieces_g[sweep, i] = pack[2 * i : 2 * i + 2]
        grams_b[sweep, chip] = pieces_g[sweep, col]
        for z in chip_peers:
            send(grams_b.at[sweep, chip], grams_b.at[sweep, chip], sweep, 5, device_on_row(z, core))
        total = mttkrp(a, high, low)
        part_b[sweep, 0] = total[:, :128]
        part_b[sweep, 1] = total[:, 128:]
        send(part_b.at[sweep, 1 - core], pair_b.at[sweep], sweep, 4, sibling)
        arrived(pair_b.at[sweep], sweep, 4)
        half_b[sweep] = (part_b[sweep, core] + pair_b[sweep]).reshape(8, 8, 128)
        for z in chip_peers:
            send(half_b.at[sweep, lax.rem(z, 8)], sums_b.at[sweep, chip], sweep, 6, device_on_row(z, core))
        sums_b[sweep, chip] = half_b[sweep, tile]
        arrived(grams_b.at[sweep, pl.ds(0, 15)], sweep, 5)
        full_g[sweep, core * COLS + col] = added(grams_b, sweep)
        piece = full_g.at[sweep, core * COLS + col]
        for x, y in col_peers:
            for c in (0, 1):
                send(piece, piece, sweep, 7, device_across(x, y, c))
        send(piece, piece, sweep, 7, sibling)
        arrived(sums_b.at[sweep, pl.ds(0, 15)], sweep, 6)
        full_b[sweep, core, tile] = added(sums_b, sweep)
        for offset in WINDOW:
            z = at_chip(offset * (1 - 2 * core))
            own = full_b.at[sweep, core, tile]
            send(own, own, sweep, 8, device_on_row(z, 1 - core))
            if offset:
                send(own, own, sweep, 8, device_on_row(z, core))
        arrived(full_g.at[sweep, pl.ds(0, 31)], sweep, 7)
        pack = jnp.concatenate([full_g[sweep, i] + full_g[sweep, COLS + i] for i in range(COLS)], axis=0)
        gram = unpacked(pack)
        scales = scales_row(gram, rows_all)
        across = 1.0 / scales
        down = 1.0 / scales_column(gram, rows_all)

        @pl.when(sweep == SWEEPS - 1)
        def _():
            out_scales[0:1, :] = scales
            out_a[...] = a * down

        system = gram_c[...] * (gram * down * across) + rows_all * eye
        solver = eliminate(jnp.concatenate([system, eye * across], axis=1))
        arrived(sums_b.at[sweep, pl.ds(0, 15)], sweep, 8)
        summed = jnp.concatenate([full_b[sweep, 0].reshape(64, 128), full_b[sweep, 1].reshape(64, 128)], axis=1)

        @pl.when(sweep < SWEEPS - 1)
        def _():
            b = jnp.dot(solver, summed, precision=HIGHEST, preferred_element_type=F32)
            keep_part_a(sweep + 1, mttkrp(b, high_t, low_t))
            keep_gram_a(sweep + 1, b)

        @pl.when(sweep == SWEEPS - 1)
        def _():
            solved_b[...] = jnp.dot(solver, summed, precision=HIGHEST, preferred_element_type=F32)

        return carry

    lax.fori_loop(0, SWEEPS, sweep_body, 0)

    b = solved_b[...]
    own = jnp.sum(gram_of(b) * eye, axis=0, keepdims=True)
    squares[col] = jnp.concatenate([own, own], axis=1)
    for x, y in col_peers:
        pltpu.make_async_remote_copy(
            src_ref=squares.at[col], dst_ref=squares.at[col], send_sem=last_send, recv_sem=last_recv,
            device_id=device_on_col(x, y), device_id_type=MESH,
        ).start()
    pltpu.make_async_copy(squares.at[pl.ds(0, 15)], squares.at[pl.ds(0, 15)], last_recv).wait()
    total = squares[0]
    for source in range(1, COLS):
        total = total + squares[source]
    scales = jnp.sqrt(total[:, :64] / cols_all + EPSILON)
    out_scales[1:2, :] = scales
    out_b[...] = b / jnp.sum(eye * scales, axis=1, keepdims=True)

    def drain(sweep, carry):
        left(grams_a.at[sweep, pl.ds(0, 15)], sweep, 0)
        left(sums_a.at[sweep, pl.ds(0, 15)], sweep, 1)
        left(full_a.at[sweep, pl.ds(0, 15)], sweep, 2)
        left(pair_b.at[sweep], sweep, 4)
        left(grams_b.at[sweep, pl.ds(0, 15)], sweep, 5)
        left(sums_b.at[sweep, pl.ds(0, 15)], sweep, 6)
        left(full_g.at[sweep, pl.ds(0, 31)], sweep, 7)
        left(sums_b.at[sweep, pl.ds(0, 15)], sweep, 8)
        left(whole_g.at[sweep, 0], sweep, 9)
        return carry

    lax.fori_loop(0, SWEEPS, drain, 0)
    pltpu.make_async_copy(squares.at[pl.ds(0, 15)], squares.at[pl.ds(0, 15)], last_send).wait()


def place(a, b, scales, out_a, out_b, out_scales):
    out_a[...] = a[...]
    out_b[...] = b[...]
    out_scales[...] = scales[...]


def shards(tensor, factor_b, factor_c):
    vmem = pl.BlockSpec(memory_space=pltpu.VMEM)
    whole = pl.BlockSpec(memory_space=pl.ANY)
    n = SWEEPS
    outs = (
        jax.ShapeDtypeStruct((64, 256), F32),
        jax.ShapeDtypeStruct((64, 256), F32),
        jax.ShapeDtypeStruct((2, 64), F32),
    )
    results = pl.pallas_call(
        kernel,
        out_shape=outs,
        in_specs=[whole, whole, whole],
        out_specs=(vmem, vmem, vmem),
        scratch_shapes=[
            pltpu.VMEM((16, 256, 256), F32),
            pltpu.VMEM((16, 256, 256), BF16),
            pltpu.VMEM((16, 256, 256), BF16),
            pltpu.VMEM((16, 256, 256), BF16),
            pltpu.VMEM((16, 256, 256), BF16),
            pltpu.VMEM((16, 64, 128), F32),
            pltpu.VMEM((16, 128), F32),
            pltpu.VMEM((64, 64), F32),
            pltpu.VMEM((64, 256), F32),
            pltpu.VMEM((n, 16, 8, 128), F32),
            pltpu.VMEM((n, 16, 8, 128), F32),
            pltpu.VMEM((n, 16, 8, 128), F32),
            pltpu.VMEM((n, 16, 16, 128), F32),
            pltpu.VMEM((n, 2, 64, 128), F32),
            pltpu.VMEM((n, 64, 128), F32),
            pltpu.VMEM((n, 8, 8, 128), F32),
            pltpu.VMEM((n, 16, 8, 128), F32),
            pltpu.VMEM((n, 2, 8, 8, 128), F32),
            pltpu.VMEM((n, 2, 16, 128), F32),
            pltpu.VMEM((n, 16, 2, 128), F32),
            pltpu.VMEM((n, 16, 2, 128), F32),
            pltpu.VMEM((n, 32, 2, 128), F32),
            pltpu.VMEM((16, 1, 128), F32),
            pltpu.VMEM((16, 64), F32),
            pltpu.SemaphoreType.DMA((2,)),
            pltpu.SemaphoreType.DMA((16,)),
            pltpu.SemaphoreType.DMA((n, 10)),
            pltpu.SemaphoreType.DMA((n, 10)),
            pltpu.SemaphoreType.DMA,
            pltpu.SemaphoreType.DMA,
        ],
        compiler_params=pltpu.CompilerParams(collective_id=0, has_side_effects=True, vmem_limit_bytes=54 * 2**20),
        name="sweeps",
    )(tensor, factor_b, factor_c)
    return pl.pallas_call(
        place,
        out_shape=outs,
        in_specs=[vmem] * 3,
        out_specs=(vmem, vmem, vmem),
        compiler_params=pltpu.CompilerParams(vmem_limit_bytes=54 * 2**20),
        name="place",
    )(*results)


def solution(mesh):
    in_specs = (P(None, "row", "col"), P(None, "col"), P())
    out_specs = (P(None, "row"), P(None, "col"), P())
    return jax.shard_map(shards, mesh=mesh, in_specs=in_specs, out_specs=out_specs, check_vma=False)
```
